32 devices in a mesh: wide: 8 (over z, core), narrow: 4 (over y, x).
Axes of the slice: x: 2, y: 2, z: 4, core: 2. Of those that a mesh axis runs over, the one named last changes fastest.
Arguments:
- state: float32 [2, 4194304], P(None, ('wide', 'narrow')), may hold values from -6 to 6
- gates: float32 [4, 2, 128, 128], replicated, may hold values from -0.375 to 0.375
- phase_index: int32 [3, 128], replicated, may hold values from 0 to 255
Outputs:
- final_state: float32 [2, 4194304], P(None, ('wide', 'narrow'))
The draws below stay inside these ranges and needn't reach their ends.
All inputs are finite; a program needn't handle non-finite values.
Results may differ from the reference program's by a relative error of at most 0.00007.
Values sent between devices are 32-bit elements; how exact they have to be, the bound alone decides.
A program may use at most 64 MiB of HBM per device.

```python
import math
import jax
import jax.numpy as jnp
from jax import lax

GATE = 128
LAYERS = 4
AMPS = 4194304
N_WIDE = 8
N_NARROW = 4


def plant(drawn, stream_key, low, largest):
    extent = drawn.shape
    spot = [jax.random.randint(jax.random.fold_in(stream_key, axis), (), 0, extent[axis]) for axis in range(len(extent))]
    drawn = drawn.at[tuple(spot)].set(low)
    longest = extent.index(max(extent))
    spot[longest] = (spot[longest] + 1) % extent[longest]
    return drawn.at[tuple(spot)].set(largest)


def shard_levels(stream_key, dims, cuts, least, largest):
    factor_of = 1.0
    for axis_at, shards_of in cuts:
        heights = jax.random.uniform(jax.random.fold_in(jax.random.fold_in(stream_key, 6), axis_at), (shards_of,), jnp.float32, least / len(cuts), largest / len(cuts))
        factor_of = factor_of * jnp.repeat(jnp.exp(heights), dims[axis_at] // shards_of).reshape((-1,) + (1,) * (len(dims) - 1 - axis_at))
    return factor_of


def scatter_about(own_key, extent, width, reach, split=(), dtype=jnp.bfloat16):
    loudness = shard_levels(own_key, extent, split, -0.22, 0.18) if split else 1.0
    entries = jax.random.normal(own_key, extent, jnp.float32) * width * loudness
    return jnp.minimum(jnp.maximum(entries, -reach), reach).astype(dtype)


def setup_inputs(seed: int = 0) -> dict:
    key_list = jax.random.split(jax.random.key(seed), 4)
    state = scatter_about(key_list[0], (2, AMPS), 1.0, 6.0, ((1, 32),), jnp.float32)
    gates = scatter_about(key_list[1], (LAYERS, 2, GATE, GATE), (2 * GATE) ** -0.5, 0.375, (), jnp.float32)
    phase_index = plant(jax.random.randint(key_list[2], (3, GATE), 0, 256), jax.random.fold_in(key_list[2], 1), 0, 255).astype(jnp.int32)
    return dict(state=state, gates=gates, phase_index=phase_index)


angle_step = 2.0 * math.pi / 256.0


def real_form(gate_re, gate_im):
    upper = jnp.stack([gate_re, -gate_im], axis=1)
    lower = jnp.stack([gate_im, gate_re], axis=1)
    return jnp.stack([upper, lower], axis=0)


def apply_last(blocks, amplitudes):
    return jnp.einsum("pmqn,qrn->prm", blocks, amplitudes, precision=lax.Precision.HIGHEST)


def apply_middle(blocks, amplitudes):
    return jnp.einsum("pmqn,qbnc->pbmc", blocks, amplitudes, precision=lax.Precision.HIGHEST)


def rotate(amplitudes, angle_sum):
    angles = angle_sum.astype(jnp.float32) * angle_step
    cosine = jnp.cos(angles)
    sine = jnp.sin(angles)
    real_part = amplitudes[0] * cosine - amplitudes[1] * sine
    imag_part = amplitudes[0] * sine + amplitudes[1] * cosine
    return jnp.stack([real_part, imag_part], axis=0)


def reference(state, gates, phase_index):
    row_count = AMPS // GATE
    local_amps = AMPS // (N_WIDE * N_NARROW)
    half_gate = GATE // 2
    amps = apply_last(real_form(gates[0, 0], gates[0, 1]), state.reshape(2, row_count, GATE))
    amps = apply_middle(real_form(gates[1, 0], gates[1, 1]), amps.reshape(2, AMPS // (GATE * GATE), GATE, GATE))
    row_ids = lax.iota(jnp.int32, row_count)
    middle_part = phase_index[1][row_ids % GATE]
    top_part = phase_index[2][row_ids // (AMPS // (GATE * GATE))]
    angle_sum = phase_index[0][None, :] + (middle_part + top_part)[:, None]
    amps = rotate(amps.reshape(2, row_count, GATE), angle_sum)
    moved = amps.reshape(2, N_WIDE, N_NARROW, N_NARROW, local_amps // N_NARROW).swapaxes(2, 3)
    moved = apply_middle(real_form(gates[2, 0], gates[2, 1]), moved.reshape(2, N_WIDE * N_NARROW, GATE, local_amps // GATE))
    blocks = real_form(gates[3, 0], gates[3, 1]).reshape(2, 2, half_gate, 2, 2, half_gate)
    grouped = moved.reshape(2, 2, N_WIDE * N_NARROW // 2, 2, half_gate, local_amps // GATE)
    moved = jnp.einsum("oxmiyn,iydtnr->oxdtmr", blocks, grouped, precision=lax.Precision.HIGHEST)
    back = moved.reshape(2, N_WIDE, N_NARROW, N_NARROW, local_amps // N_NARROW).swapaxes(2, 3)
    return back.reshape(2, AMPS)
```

```python
import functools
import math

import jax
import jax.numpy as jnp
from jax import lax
from jax.experimental import pallas as pl
from jax.experimental.pallas import tpu as pltpu
from jax.sharding import PartitionSpec as P

GATE = 128

angle_step = 2.0 * math.pi / 256.0


def split(value):
    high = value.astype(jnp.bfloat16)
    low = (value - high.astype(jnp.float32)).astype(jnp.bfloat16)
    return high, low


def product(left, right):
    (left_high, left_low), (right_high, right_low) = left, right
    dot = functools.partial(jnp.dot, preferred_element_type=jnp.float32)
    return dot(left_high, right_high) + (dot(left_high, right_low) + dot(left_low, right_high))


def real_form(gate_re, gate_im):
    upper = jnp.concatenate([gate_re, -gate_im], axis=1)
    lower = jnp.concatenate([gate_im, gate_re], axis=1)
    return jnp.concatenate([upper, lower], axis=0)


def kernel(
    dims,
    x_ref,
    gates_ref,
    phase_ref,
    out_ref,
    amps,
    gate_rows,
    spread,
    gathered,
    finished,
    returned,
    own_sem,
    swap_send,
    swap_recv,
    spread_send,
    spread_recv,
    return_send,
    return_recv,
):
    wide_count, narrow_count, chunk_count, free, extra, inner, low, per_dest, top_span = dims
    wide = lax.axis_index("wide")
    me = lax.axis_index("narrow")
    side = wide // (wide_count // 2)
    partner = lax.rem(wide + wide_count // 2, wide_count)
    sides = (wide, partner)
    half = GATE // 2

    def swap(c):
        return pltpu.make_async_remote_copy(
            src_ref=x_ref.at[1 - side, c],
            dst_ref=amps.at[1, c],
            send_sem=swap_send.at[c],
            recv_sem=swap_recv.at[c],
            device_id=(partner, me),
            device_id_type=pl.DeviceIdType.MESH,
        )

    def spread_copy(slot, f, d):
        dest = lax.rem(me + d, narrow_count)
        return pltpu.make_async_remote_copy(
            src_ref=spread.at[slot, f, dest],
            dst_ref=gathered.at[slot, f, me],
            send_sem=spread_send.at[slot, f, d],
            recv_sem=spread_recv.at[slot, f, me],
            device_id=(wide, dest),
            device_id_type=pl.DeviceIdType.MESH,
        )

    def spread_arrival(slot, f, d):
        source = lax.rem(me + d, narrow_count)
        return pltpu.make_async_remote_copy(
            src_ref=spread.at[slot, f, source],
            dst_ref=gathered.at[slot, f, source],
            send_sem=spread_send.at[slot, f, d],
            recv_sem=spread_recv.at[slot, f, source],
            device_id=(wide, source),
            device_id_type=pl.DeviceIdType.MESH,
        )

    def return_copy(slot, f, d):
        dest = lax.rem(me + d, narrow_count)
        return pltpu.make_async_remote_copy(
            src_ref=finished.at[slot, f, dest],
            dst_ref=returned.at[slot, f, me],
            send_sem=return_send.at[slot, f, d],
            recv_sem=return_recv.at[slot, f, me],
            device_id=(sides[slot], dest),
            device_id_type=pl.DeviceIdType.MESH,
        )

    def return_arrival(slot, f, d):
        source = lax.rem(me + d, narrow_count)
        return pltpu.make_async_remote_copy(
            src_ref=finished.at[slot, f, source],
            dst_ref=returned.at[slot, f, source],
            send_sem=return_send.at[slot, f, d],
            recv_sem=return_recv.at[slot, f, source],
            device_id=(sides[slot], source),
            device_id_type=pl.DeviceIdType.MESH,
        )

    own = pltpu.make_async_copy(x_ref.at[side], amps.at[0], own_sem)
    own.start()
    barrier = pltpu.get_barrier_semaphore()
    for slot in range(2):
        for d in range(1 - slot, narrow_count):
            peer = lax.rem(me + d, narrow_count)
            pl.semaphore_signal(
                barrier, inc=1, device_id=(sides[slot], peer), device_id_type=pl.DeviceIdType.MESH
            )
    pl.semaphore_wait(barrier, 2 * narrow_count - 1)
    window = min(2, chunk_count)
    for c in range(window):
        swap(c).start()

    cos_low, sin_low = phase_ref[0:1, :], phase_ref[3:4, :]
    re, im = gates_ref[0, 0].T, gates_ref[0, 1].T
    re, im = re * cos_low - im * sin_low, re * sin_low + im * cos_low
    upper = jnp.concatenate([re, im], axis=1)
    lower = jnp.concatenate([-im, re], axis=1)
    lane_gate = split(jnp.concatenate([upper, lower], axis=0))

    cos_mid = jnp.broadcast_to(phase_ref[1:2, :], (GATE, GATE)).T
    sin_mid = jnp.broadcast_to(phase_ref[4:5, :], (GATE, GATE)).T
    re, im = gates_ref[1, 0], gates_ref[1, 1]
    gate_rows[0] = re * cos_mid - im * sin_mid
    gate_rows[1] = re * sin_mid + im * cos_mid

    def row_start(s):
        return (s // low) * low * inner + s % low

    settings = GATE // inner
    re, im = [
        jnp.concatenate(
            [gate_rows[p, pl.ds(row_start(s), inner, stride=low), :] for s in range(settings)], axis=0
        )
        for p in range(2)
    ]
    row_gate = split(real_form(re, im))

    lanes = lax.broadcasted_iota(jnp.int32, (1, GATE), 1)

    def first_gates(slot, c):
        x = jnp.concatenate([amps[slot, c, pl.ds(p, GATE, stride=2), :] for p in range(2)], axis=0)
        y = product(row_gate, split(x))
        y = jnp.concatenate([y[:GATE], y[GATE:]], axis=1)
        y = product(split(y), lane_gate)
        re, im = y[:, :GATE], y[:, GATE:]
        device = sides[slot] * narrow_count + me
        top = ((device * 2 + side) * chunk_count + c) // top_span
        cos_top = jnp.sum(jnp.where(lanes == top, phase_ref[2:3, :], 0.0), axis=1, keepdims=True)
        sin_top = jnp.sum(jnp.where(lanes == top, phase_ref[5:6, :], 0.0), axis=1, keepdims=True)
        f, e = c // extra, c % extra
        shape = (narrow_count, per_dest * inner, GATE)
        spread[slot, f, :, e, 0] = (re * cos_top - im * sin_top).reshape(shape)
        spread[slot, f, :, e, 1] = (re * sin_top + im * cos_top).reshape(shape)
        if e == extra - 1:
            for d in range(1, narrow_count):
                spread_copy(slot, f, d).start()
            gathered[slot, f, me] = spread[slot, f, me]

    own.wait()
    for c in range(chunk_count):
        first_gates(0, c)

    third_gate = split(real_form(gates_ref[2, 0], gates_ref[2, 1]))

    def by_side(gate):
        turned = jnp.concatenate([gate[:, half:], gate[:, :half]], axis=1)
        turned = jnp.concatenate([turned[half:], turned[:half]], axis=0)
        return jnp.where(side == 0, gate, turned)

    fourth_gate = split(real_form(by_side(gates_ref[3, 0]), by_side(gates_ref[3, 1])))

    def last_gates(f):
        ys = []
        for slot in range(2):
            for d in range(1, narrow_count):
                spread_arrival(slot, f, d).wait_recv()
            columns = [
                jnp.concatenate(
                    [
                        gathered[slot, f, n, e, p, u * inner : (u + 1) * inner, :]
                        for p in range(2)
                        for n in range(narrow_count)
                        for e in range(extra)
                    ],
                    axis=0,
                )
                for u in range(per_dest)
            ]
            x = jnp.concatenate(columns, axis=1) if per_dest > 1 else columns[0]
            ys.append(product(third_gate, split(x)))
        for t in range(2):
            x = jnp.concatenate(
                [
                    ys[slot][p * GATE + t * half : p * GATE + (t + 1) * half]
                    for p in range(2)
                    for slot in range(2)
                ],
                axis=0,
            )
            z = product(fourth_gate, split(x))
            for slot in range(2):
                for n in range(narrow_count // 2):
                    for e in range(extra):
                        for p in range(2):
                            row = p * GATE + slot * half + (n * extra + e) * inner
                            for u in range(per_dest):
                                finished[
                                    slot, f, t * (narrow_count // 2) + n, e, p, u * inner : (u + 1) * inner, :
                                ] = z[row : row + inner, u * GATE : (u + 1) * GATE]
        for slot in (1, 0):
            for d in range(1 - slot, narrow_count):
                return_copy(slot, f, d).start()
        returned[0, f, me] = finished[0, f, me]

    for c in range(chunk_count):
        swap(c).wait_recv()
        if c + window < chunk_count:
            swap(c + window).start()
        first_gates(1, c)
        if c % extra == extra - 1:
            last_gates(c // extra)

    for f in range(free):
        for slot in range(2):
            for d in range(1 - slot, narrow_count):
                return_arrival(slot, f, d).wait_recv()
            origin = side if slot == 0 else 1 - side
            for n in range(narrow_count):
                for e in range(extra):
                    for p in range(2):
                        for u in range(per_dest):
                            row = 2 * row_start(n * per_dest + u) + p
                            out_ref[origin, f * extra + e, pl.ds(row, inner, stride=2 * low), :] = returned[
                                slot, f, n, e, p, u * inner : (u + 1) * inner, :
                            ]

    for c in range(chunk_count):
        swap(c).wait_send()
    for f in range(free):
        for slot in range(2):
            for d in range(1, narrow_count):
                spread_copy(slot, f, d).wait_send()
            for d in range(1 - slot, narrow_count):
                return_copy(slot, f, d).wait_send()


def local(state, gates, phase_index):
    local_amps = state.shape[1]
    narrow_count = lax.axis_size("narrow")
    wide_count = lax.axis_size("wide")
    rows = local_amps // GATE
    low = rows // GATE
    chunk_count = local_amps // (2 * GATE * GATE)
    contracted = GATE // narrow_count
    inner = min(contracted, GATE // low)
    extra = contracted // inner
    free = chunk_count // extra
    per_dest = GATE // inner // narrow_count
    top_span = local_amps * wide_count * narrow_count // GATE**3
    dims = (wide_count, narrow_count, chunk_count, free, extra, inner, low, per_dest, top_span)
    angles = phase_index.astype(jnp.float32) * angle_step
    phases = jnp.concatenate([jnp.cos(angles), jnp.sin(angles)], axis=0)
    x = state.reshape(2, rows, GATE).transpose(1, 0, 2).reshape(2, chunk_count, 2 * GATE, GATE)
    vmem = pl.BlockSpec(memory_space=pltpu.VMEM)
    message = pltpu.VMEM((2, free, narrow_count, extra, 2, per_dest * inner, GATE), jnp.float32)
    pair_sems = pltpu.SemaphoreType.DMA((2, free, narrow_count))
    flops = 4 * 2 * (2 * GATE) ** 2 * rows * 3
    out = pl.pallas_call(
        functools.partial(kernel, dims),
        out_shape=jax.ShapeDtypeStruct(x.shape, jnp.float32),
        in_specs=[pl.BlockSpec(memory_space=pl.ANY), vmem, vmem],
        out_specs=vmem,
        scratch_shapes=[
            pltpu.VMEM(x.shape, jnp.float32),
            pltpu.VMEM((2, GATE, GATE), jnp.float32),
            message,
            message,
            message,
            message,
            pltpu.SemaphoreType.DMA,
            pltpu.SemaphoreType.DMA((chunk_count,)),
            pltpu.SemaphoreType.DMA((chunk_count,)),
            pair_sems,
            pair_sems,
            pair_sems,
            pair_sems,
        ],
        compiler_params=pltpu.CompilerParams(
            collective_id=0, has_side_effects=True, vmem_limit_bytes=32 * 2**20
        ),
        cost_estimate=pl.CostEstimate(flops=flops, bytes_accessed=4 * local_amps * 4, transcendentals=0),
    )(x, gates, phases)
    return out.reshape(rows, 2, GATE).transpose(1, 0, 2).reshape(2, local_amps)


def solution(mesh):
    in_specs = (P(None, ("wide", "narrow")), P(), P())
    out_specs = P(None, ("wide", "narrow"))
    return jax.shard_map(local, mesh=mesh, in_specs=in_specs, out_specs=out_specs, check_vma=False)
```

```python
import functools
import math

import jax
import jax.numpy as jnp
from jax import lax
from jax.experimental import pallas as pl
from jax.experimental.pallas import tpu as pltpu
from jax.sharding import PartitionSpec as P

GATE = 128

angle_step = 2.0 * math.pi / 256.0


def split(value):
    high = value.astype(jnp.bfloat16)
    low = (value - high.astype(jnp.float32)).astype(jnp.bfloat16)
    return high, low


def product(left, right):
    (left_high, left_low), (right_high, right_low) = left, right
    dot = functools.partial(jnp.dot, preferred_element_type=jnp.float32)
    return dot(left_high, right_high) + (dot(left_high, right_low) + dot(left_low, right_high))


def real_form(gate_re, gate_im):
    upper = jnp.concatenate([gate_re, -gate_im], axis=1)
    lower = jnp.concatenate([gate_im, gate_re], axis=1)
    return jnp.concatenate([upper, lower], axis=0)


def kernel(
    dims,
    x_ref,
    gates_in,
    phase_index_ref,
    out_ref,
    amps,
    gates_ref,
    gate_rows,
    spread,
    gathered,
    finished,
    returned,
    own_sem,
    gates_sem,
    swap_send,
    swap_recv,
    spread_send,
    spread_recv,
    return_send,
    return_recv,
    credit,
):
    wide_count, narrow_count, chunk_count, free, extra, inner, low, per_dest, top_span = dims
    wide = lax.axis_index("wide")
    me = lax.axis_index("narrow")
    side = wide // (wide_count // 2)
    partner = lax.rem(wide + wide_count // 2, wide_count)
    sides = (wide, partner)
    quarter = wide_count // 4
    cross = wide + quarter * (1 - 2 * lax.rem(wide // quarter, 2))
    half = GATE // 2

    def swap(c):
        return pltpu.make_async_remote_copy(
            src_ref=x_ref.at[1 - side, c],
            dst_ref=amps.at[1, c],
            send_sem=swap_send.at[c],
            recv_sem=swap_recv.at[c],
            device_id=(partner, me),
            device_id_type=pl.DeviceIdType.MESH,
        )

    def spread_copy(slot, f, d):
        dest = lax.rem(me + d, narrow_count)
        return pltpu.make_async_remote_copy(
            src_ref=spread.at[slot, f, dest],
            dst_ref=gathered.at[slot, f, me],
            send_sem=spread_send.at[slot, f, d],
            recv_sem=spread_recv.at[slot, f, me],
            device_id=(wide, dest),
            device_id_type=pl.DeviceIdType.MESH,
        )

    def spread_arrival(slot, f, d):
        source = lax.rem(me + d, narrow_count)
        return pltpu.make_async_remote_copy(
            src_ref=spread.at[slot, f, source],
            dst_ref=gathered.at[slot, f, source],
            send_sem=spread_send.at[slot, f, d],
            recv_sem=spread_recv.at[slot, f, source],
            device_id=(wide, source),
            device_id_type=pl.DeviceIdType.MESH,
        )

    def return_copy(slot, f, d):
        dest = lax.rem(me + d, narrow_count)
        return pltpu.make_async_remote_copy(
            src_ref=finished.at[slot, f, dest],
            dst_ref=returned.at[slot, f, me],
            send_sem=return_send.at[slot, f, d],
            recv_sem=return_recv.at[slot, f, me],
            device_id=(sides[slot], dest),
            device_id_type=pl.DeviceIdType.MESH,
        )

    def return_arrival(slot, f, d):
        source = lax.rem(me + d, narrow_count)
        return pltpu.make_async_remote_copy(
            src_ref=finished.at[slot, f, source],
            dst_ref=returned.at[slot, f, source],
            send_sem=return_send.at[slot, f, d],
            recv_sem=return_recv.at[slot, f, source],
            device_id=(sides[slot], source),
            device_id_type=pl.DeviceIdType.MESH,
        )

    own = pltpu.make_async_copy(x_ref.at[side], amps.at[0], own_sem)
    own.start()
    gates_copy = pltpu.make_async_copy(gates_in, gates_ref, gates_sem)
    gates_copy.start()
    barrier = pltpu.get_barrier_semaphore()
    for slot in range(2):
        for d in range(1 - slot, narrow_count):
            peer = lax.rem(me + d, narrow_count)
            pl.semaphore_signal(
                barrier, inc=1, device_id=(sides[slot], peer), device_id_type=pl.DeviceIdType.MESH
            )
    pl.semaphore_signal(barrier, inc=1, device_id=(cross, me), device_id_type=pl.DeviceIdType.MESH)
    pl.semaphore_wait(barrier, 2 * narrow_count)
    window = min(2, chunk_count)
    for c in range(window):
        swap(c).start()

    angles = phase_index_ref[...].astype(jnp.float32) * angle_step
    cosine, sine = jnp.cos(angles), jnp.sin(angles)
    gates_copy.wait()

    cos_low, sin_low = cosine[0:1, :], sine[0:1, :]
    re, im = gates_ref[0, 0].T, gates_ref[0, 1].T
    re, im = re * cos_low - im * sin_low, re * sin_low + im * cos_low
    upper = jnp.concatenate([re, im], axis=1)
    lower = jnp.concatenate([-im, re], axis=1)
    lane_gate = split(jnp.concatenate([upper, lower], axis=0))

    cos_mid = jnp.broadcast_to(cosine[1:2, :], (GATE, GATE)).T
    sin_mid = jnp.broadcast_to(sine[1:2, :], (GATE, GATE)).T
    re, im = gates_ref[1, 0], gates_ref[1, 1]
    gate_rows[0] = re * cos_mid - im * sin_mid
    gate_rows[1] = re * sin_mid + im * cos_mid

    def row_start(s):
        return (s // low) * low * inner + s % low

    settings = GATE // inner
    re, im = [
        jnp.concatenate(
            [gate_rows[p, pl.ds(row_start(s), inner, stride=low), :] for s in range(settings)], axis=0
        )
        for p in range(2)
    ]
    row_gate = split(real_form(re, im))

    lanes = lax.broadcasted_iota(jnp.int32, (1, GATE), 1)

    def first_gates(slot, c):
        x = jnp.concatenate([amps[slot, c, pl.ds(p, GATE, stride=2), :] for p in range(2)], axis=0)
        y = product(row_gate, split(x))
        y = jnp.concatenate([y[:GATE], y[GATE:]], axis=1)
        y = product(split(y), lane_gate)
        re, im = y[:, :GATE], y[:, GATE:]
        device = sides[slot] * narrow_count + me
        top = ((device * 2 + side) * chunk_count + c) // top_span
        cos_top = jnp.sum(jnp.where(lanes == top, cosine[2:3, :], 0.0), axis=1, keepdims=True)
        sin_top = jnp.sum(jnp.where(lanes == top, sine[2:3, :], 0.0), axis=1, keepdims=True)
        f, e = c // extra, c % extra
        shape = (narrow_count, per_dest * inner, GATE)
        spread[slot, f, :, e, 0] = (re * cos_top - im * sin_top).reshape(shape)
        spread[slot, f, :, e, 1] = (re * sin_top + im * cos_top).reshape(shape)
        if e == extra - 1:
            for d in range(1, narrow_count):
                spread_copy(slot, f, d).start()
            gathered[slot, f, me] = spread[slot, f, me]

    own.wait()
    for c in range(chunk_count):
        first_gates(0, c)

    third_gate = split(real_form(gates_ref[2, 0], gates_ref[2, 1]))

    def by_side(gate):
        turned = jnp.concatenate([gate[:, half:], gate[:, :half]], axis=1)
        turned = jnp.concatenate([turned[half:], turned[:half]], axis=0)
        return jnp.where(side == 0, gate, turned)

    fourth_gate = split(real_form(by_side(gates_ref[3, 0]), by_side(gates_ref[3, 1])))

    def last_gates(f):
        ys = []
        for slot in range(2):
            for d in range(1, narrow_count):
                spread_arrival(slot, f, d).wait_recv()
            columns = [
                jnp.concatenate(
                    [
                        gathered[slot, f, n, e, p, u * inner : (u + 1) * inner, :]
                        for p in range(2)
                        for n in range(narrow_count)
                        for e in range(extra)
                    ],
                    axis=0,
                )
                for u in range(per_dest)
            ]
            x = jnp.concatenate(columns, axis=1) if per_dest > 1 else columns[0]
            ys.append(product(third_gate, split(x)))
        for t in range(2):
            x = jnp.concatenate(
                [
                    ys[slot][p * GATE + t * half : p * GATE + (t + 1) * half]
                    for p in range(2)
                    for slot in range(2)
                ],
                axis=0,
            )
            z = product(fourth_gate, split(x))
            for slot in range(2):
                for n in range(narrow_count // 2):
                    for e in range(extra):
                        for p in range(2):
                            row = p * GATE + slot * half + (n * extra + e) * inner
                            for u in range(per_dest):
                                finished[
                                    slot, f, t * (narrow_count // 2) + n, e, p, u * inner : (u + 1) * inner, :
                                ] = z[row : row + inner, u * GATE : (u + 1) * GATE]
        for d in range(1, narrow_count):
            return_copy(0, f, d).start()
        returned[0, f, me] = finished[0, f, me]

    waiting = []
    for c in range(chunk_count):
        swap(c).wait_recv()
        last = c == chunk_count - 1
        if not last:
            pl.semaphore_signal(credit, inc=1, device_id=(cross, me), device_id_type=pl.DeviceIdType.MESH)
        first_gates(1, c)
        if not last:
            pl.semaphore_wait(credit, 1)
            if c + window < chunk_count:
                swap(c + window).start()
        if c % extra == extra - 1:
            last_gates(c // extra)
            waiting.append(c // extra)
        if c >= chunk_count - 2:
            for f in waiting:
                for d in range(narrow_count):
                    return_copy(1, f, d).start()
            waiting = []

    for f in range(free):
        for slot in range(2):
            for d in range(1 - slot, narrow_count):
                return_arrival(slot, f, d).wait_recv()
            origin = side if slot == 0 else 1 - side
            for n in range(narrow_count):
                for e in range(extra):
                    for p in range(2):
                        for u in range(per_dest):
                            row = 2 * row_start(n * per_dest + u) + p
                            out_ref[origin, f * extra + e, pl.ds(row, inner, stride=2 * low), :] = returned[
                                slot, f, n, e, p, u * inner : (u + 1) * inner, :
                            ]

    for c in range(chunk_count):
        swap(c).wait_send()
    for f in range(free):
        for slot in range(2):
            for d in range(1, narrow_count):
                spread_copy(slot, f, d).wait_send()
            for d in range(1 - slot, narrow_count):
                return_copy(slot, f, d).wait_send()


def local(state, gates, phase_index):
    local_amps = state.shape[1]
    narrow_count = lax.axis_size("narrow")
    wide_count = lax.axis_size("wide")
    rows = local_amps // GATE
    low = rows // GATE
    chunk_count = local_amps // (2 * GATE * GATE)
    contracted = GATE // narrow_count
    inner = min(contracted, GATE // low)
    extra = contracted // inner
    free = chunk_count // extra
    per_dest = GATE // inner // narrow_count
    top_span = local_amps * wide_count * narrow_count // GATE**3
    dims = (wide_count, narrow_count, chunk_count, free, extra, inner, low, per_dest, top_span)
    x = state.reshape(2, rows, GATE).transpose(1, 0, 2).reshape(2, chunk_count, 2 * GATE, GATE)
    vmem = pl.BlockSpec(memory_space=pltpu.VMEM)
    hbm = pl.BlockSpec(memory_space=pltpu.HBM)
    message = pltpu.VMEM((2, free, narrow_count, extra, 2, per_dest * inner, GATE), jnp.float32)
    pair_sems = pltpu.SemaphoreType.DMA((2, free, narrow_count))
    flops = 4 * 2 * (2 * GATE) ** 2 * rows * 3
    out = pl.pallas_call(
        functools.partial(kernel, dims),
        out_shape=jax.ShapeDtypeStruct(x.shape, jnp.float32),
        in_specs=[hbm, hbm, vmem],
        out_specs=vmem,
        scratch_shapes=[
            pltpu.VMEM(x.shape, jnp.float32),
            pltpu.VMEM(gates.shape, jnp.float32),
            pltpu.VMEM((2, GATE, GATE), jnp.float32),
            message,
            message,
            message,
            message,
            pltpu.SemaphoreType.DMA,
            pltpu.SemaphoreType.DMA,
            pltpu.SemaphoreType.DMA((chunk_count,)),
            pltpu.SemaphoreType.DMA((chunk_count,)),
            pair_sems,
            pair_sems,
            pair_sems,
            pair_sems,
            pltpu.SemaphoreType.REGULAR,
        ],
        compiler_params=pltpu.CompilerParams(
            collective_id=0, has_side_effects=True, vmem_limit_bytes=60 * 2**20
        ),
        cost_estimate=pl.CostEstimate(flops=flops, bytes_accessed=4 * local_amps * 4, transcendentals=0),
    )(x, gates, phase_index)
    return out.reshape(rows, 2, GATE).transpose(1, 0, 2).reshape(2, local_amps)


def solution(mesh):
    in_specs = (P(None, ("wide", "narrow")), P(), P())
    out_specs = P(None, ("wide", "narrow"))
    return jax.shard_map(local, mesh=mesh, in_specs=in_specs, out_specs=out_specs, check_vma=False)
```

```python
import functools
import math

import jax
import jax.numpy as jnp
from jax import lax
from jax.experimental import pallas as pl
from jax.experimental.pallas import tpu as pltpu
from jax.sharding import PartitionSpec as P

GATE = 128

angle_step = 2.0 * math.pi / 256.0


def split(value):
    high = value.astype(jnp.bfloat16)
    low = (value - high.astype(jnp.float32)).astype(jnp.bfloat16)
    return high, low


def product(left, right):
    (left_high, left_low), (right_high, right_low) = left, right
    dot = functools.partial(jnp.dot, preferred_element_type=jnp.float32)
    return dot(left_high, right_high) + (dot(left_high, right_low) + dot(left_low, right_high))


def real_form(gate_re, gate_im):
    upper = jnp.concatenate([gate_re, -gate_im], axis=1)
    lower = jnp.concatenate([gate_im, gate_re], axis=1)
    return jnp.concatenate([upper, lower], axis=0)


def kernel(
    dims,
    x_ref,
    gates_in,
    phase_index_ref,
    out_ref,
    amps,
    gates_ref,
    gate_rows,
    spread,
    gathered,
    finished,
    returned,
    own_sem,
    gates_sem,
    swap_send,
    swap_recv,
    spread_send,
    spread_recv,
    return_send,
    return_recv,
):
    wide_count, narrow_count, chunk_count, free, extra, inner, low, per_dest, top_span = dims
    wide = lax.axis_index("wide")
    me = lax.axis_index("narrow")
    side = wide // (wide_count // 2)
    partner = lax.rem(wide + wide_count // 2, wide_count)
    sides = (wide, partner)
    half = GATE // 2

    def swap(c):
        return pltpu.make_async_remote_copy(
            src_ref=x_ref.at[1 - side, c],
            dst_ref=amps.at[1, c],
            send_sem=swap_send.at[c],
            recv_sem=swap_recv.at[c],
            device_id=(partner, me),
            device_id_type=pl.DeviceIdType.MESH,
        )

    def spread_copy(slot, f, d):
        dest = lax.rem(me + d, narrow_count)
        return pltpu.make_async_remote_copy(
            src_ref=spread.at[slot, f, dest],
            dst_ref=gathered.at[slot, f, me],
            send_sem=spread_send.at[slot, f, d],
            recv_sem=spread_recv.at[slot, f, me],
            device_id=(wide, dest),
            device_id_type=pl.DeviceIdType.MESH,
        )

    def spread_arrival(slot, f, d):
        source = lax.rem(me + d, narrow_count)
        return pltpu.make_async_remote_copy(
            src_ref=spread.at[slot, f, source],
            dst_ref=gathered.at[slot, f, source],
            send_sem=spread_send.at[slot, f, d],
            recv_sem=spread_recv.at[slot, f, source],
            device_id=(wide, source),
            device_id_type=pl.DeviceIdType.MESH,
        )

    def return_copy(slot, f, d):
        dest = lax.rem(me + d, narrow_count)
        return pltpu.make_async_remote_copy(
            src_ref=finished.at[slot, f, dest],
            dst_ref=returned.at[slot, f, me],
            send_sem=return_send.at[slot, f, d],
            recv_sem=return_recv.at[slot, f, me],
            device_id=(sides[slot], dest),
            device_id_type=pl.DeviceIdType.MESH,
        )

    def return_arrival(slot, f, d):
        source = lax.rem(me + d, narrow_count)
        return pltpu.make_async_remote_copy(
            src_ref=finished.at[slot, f, source],
            dst_ref=returned.at[slot, f, source],
            send_sem=return_send.at[slot, f, d],
            recv_sem=return_recv.at[slot, f, source],
            device_id=(sides[slot], source),
            device_id_type=pl.DeviceIdType.MESH,
        )

    own = pltpu.make_async_copy(x_ref.at[side], amps.at[0], own_sem)
    own.start()
    gates_copy = pltpu.make_async_copy(gates_in, gates_ref, gates_sem)
    gates_copy.start()
    barrier = pltpu.get_barrier_semaphore()
    for slot in range(2):
        for d in range(1 - slot, narrow_count):
            peer = lax.rem(me + d, narrow_count)
            pl.semaphore_signal(
                barrier, inc=1, device_id=(sides[slot], peer), device_id_type=pl.DeviceIdType.MESH
            )
    pl.semaphore_wait(barrier, 2 * narrow_count - 1)
    window = min(3, chunk_count)
    for c in range(window):
        swap(c).start()

    angles = phase_index_ref[...].astype(jnp.float32) * angle_step
    cosine, sine = jnp.cos(angles), jnp.sin(angles)
    gates_copy.wait()

    cos_low, sin_low = cosine[0:1, :], sine[0:1, :]
    re, im = gates_ref[0, 0].T, gates_ref[0, 1].T
    re, im = re * cos_low - im * sin_low, re * sin_low + im * cos_low
    upper = jnp.concatenate([re, im], axis=1)
    lower = jnp.concatenate([-im, re], axis=1)
    lane_gate = split(jnp.concatenate([upper, lower], axis=0))

    cos_mid = jnp.broadcast_to(cosine[1:2, :], (GATE, GATE)).T
    sin_mid = jnp.broadcast_to(sine[1:2, :], (GATE, GATE)).T
    re, im = gates_ref[1, 0], gates_ref[1, 1]
    gate_rows[0] = re * cos_mid - im * sin_mid
    gate_rows[1] = re * sin_mid + im * cos_mid

    def row_start(s):
        return (s // low) * low * inner + s % low

    settings = GATE // inner
    re, im = [
        jnp.concatenate(
            [gate_rows[p, pl.ds(row_start(s), inner, stride=low), :] for s in range(settings)], axis=0
        )
        for p in range(2)
    ]
    row_gate = split(real_form(re, im))

    lanes = lax.broadcasted_iota(jnp.int32, (1, GATE), 1)

    def first_gates(slot, c):
        x = jnp.concatenate([amps[slot, c, pl.ds(p, GATE, stride=2), :] for p in range(2)], axis=0)
        y = product(row_gate, split(x))
        y = jnp.concatenate([y[:GATE], y[GATE:]], axis=1)
        y = product(split(y), lane_gate)
        re, im = y[:, :GATE], y[:, GATE:]
        device = sides[slot] * narrow_count + me
        top = ((device * 2 + side) * chunk_count + c) // top_span
        cos_top = jnp.sum(jnp.where(lanes == top, cosine[2:3, :], 0.0), axis=1, keepdims=True)
        sin_top = jnp.sum(jnp.where(lanes == top, sine[2:3, :], 0.0), axis=1, keepdims=True)
        f, e = c // extra, c % extra
        shape = (narrow_count, per_dest * inner, GATE)
        spread[slot, f, :, e, 0] = (re * cos_top - im * sin_top).reshape(shape)
        spread[slot, f, :, e, 1] = (re * sin_top + im * cos_top).reshape(shape)
        if e == extra - 1:
            for d in range(1, narrow_count):
                spread_copy(slot, f, d).start()
            gathered[slot, f, me] = spread[slot, f, me]

    own.wait()
    for c in range(extra):
        first_gates(0, c)

    third_gate = split(real_form(gates_ref[2, 0], gates_ref[2, 1]))

    def by_side(gate):
        turned = jnp.concatenate([gate[:, half:], gate[:, :half]], axis=1)
        turned = jnp.concatenate([turned[half:], turned[:half]], axis=0)
        return jnp.where(side == 0, gate, turned)

    fourth_gate = split(real_form(by_side(gates_ref[3, 0]), by_side(gates_ref[3, 1])))

    def last_gates(f):
        ys = []
        for slot in range(2):
            for d in range(1, narrow_count):
                spread_arrival(slot, f, d).wait_recv()
            columns = [
                jnp.concatenate(
                    [
                        gathered[slot, f, n, e, p, u * inner : (u + 1) * inner, :]
                        for p in range(2)
                        for n in range(narrow_count)
                        for e in range(extra)
                    ],
                    axis=0,
                )
                for u in range(per_dest)
            ]
            x = jnp.concatenate(columns, axis=1) if per_dest > 1 else columns[0]
            ys.append(product(third_gate, split(x)))
        for t in range(2):
            x = jnp.concatenate(
                [
                    ys[slot][p * GATE + t * half : p * GATE + (t + 1) * half]
                    for p in range(2)
                    for slot in range(2)
                ],
                axis=0,
            )
            z = product(fourth_gate, split(x))
            for slot in range(2):
                for n in range(narrow_count // 2):
                    for e in range(extra):
                        for p in range(2):
                            row = p * GATE + slot * half + (n * extra + e) * inner
                            for u in range(per_dest):
                                finished[
                                    slot, f, t * (narrow_count // 2) + n, e, p, u * inner : (u + 1) * inner, :
                                ] = z[row : row + inner, u * GATE : (u + 1) * GATE]
        for slot in (1, 0):
            for d in range(1 - slot, narrow_count):
                return_copy(slot, f, d).start()
        returned[0, f, me] = finished[0, f, me]

    for f in range(free):
        if f > 0:
            for e in range(extra):
                first_gates(0, f * extra + e)
        for e in range(extra):
            c = f * extra + e
            swap(c).wait_recv()
            if c + window < chunk_count:
                swap(c + window).start()
            first_gates(1, c)
        last_gates(f)

    for f in range(free):
        for slot in range(2):
            for d in range(1 - slot, narrow_count):
                return_arrival(slot, f, d).wait_recv()
            origin = side if slot == 0 else 1 - side
            for n in range(narrow_count):
                for e in range(extra):
                    for p in range(2):
                        for u in range(per_dest):
                            row = 2 * row_start(n * per_dest + u) + p
                            out_ref[origin, f * extra + e, pl.ds(row, inner, stride=2 * low), :] = returned[
                                slot, f, n, e, p, u * inner : (u + 1) * inner, :
                            ]

    for c in range(chunk_count):
        swap(c).wait_send()
    for f in range(free):
        for slot in range(2):
            for d in range(1, narrow_count):
                spread_copy(slot, f, d).wait_send()
            for d in range(1 - slot, narrow_count):
                return_copy(slot, f, d).wait_send()


def local(state, gates, phase_index):
    local_amps = state.shape[1]
    narrow_count = lax.axis_size("narrow")
    wide_count = lax.axis_size("wide")
    rows = local_amps // GATE
    low = rows // GATE
    chunk_count = local_amps // (2 * GATE * GATE)
    contracted = GATE // narrow_count
    inner = min(contracted, GATE // low)
    extra = contracted // inner
    free = chunk_count // extra
    per_dest = GATE // inner // narrow_count
    top_span = local_amps * wide_count * narrow_count // GATE**3
    dims = (wide_count, narrow_count, chunk_count, free, extra, inner, low, per_dest, top_span)
    x = state.reshape(2, rows, GATE).transpose(1, 0, 2).reshape(2, chunk_count, 2 * GATE, GATE)
    vmem = pl.BlockSpec(memory_space=pltpu.VMEM)
    hbm = pl.BlockSpec(memory_space=pltpu.HBM)
    message = pltpu.VMEM((2, free, narrow_count, extra, 2, per_dest * inner, GATE), jnp.float32)
    pair_sems = pltpu.SemaphoreType.DMA((2, free, narrow_count))
    flops = 4 * 2 * (2 * GATE) ** 2 * rows * 3
    out = pl.pallas_call(
        functools.partial(kernel, dims),
        out_shape=jax.ShapeDtypeStruct(x.shape, jnp.float32),
        in_specs=[hbm, hbm, vmem],
        out_specs=vmem,
        scratch_shapes=[
            pltpu.VMEM(x.shape, jnp.float32),
            pltpu.VMEM(gates.shape, jnp.float32),
            pltpu.VMEM((2, GATE, GATE), jnp.float32),
            message,
            message,
            message,
            message,
            pltpu.SemaphoreType.DMA,
            pltpu.SemaphoreType.DMA,
            pltpu.SemaphoreType.DMA((chunk_count,)),
            pltpu.SemaphoreType.DMA((chunk_count,)),
            pair_sems,
            pair_sems,
            pair_sems,
            pair_sems,
        ],
        compiler_params=pltpu.CompilerParams(
            collective_id=0, has_side_effects=True, vmem_limit_bytes=60 * 2**20
        ),
        cost_estimate=pl.CostEstimate(flops=flops, bytes_accessed=4 * local_amps * 4, transcendentals=0),
    )(x, gates, phase_index)
    return out.reshape(rows, 2, GATE).transpose(1, 0, 2).reshape(2, local_amps)


def solution(mesh):
    in_specs = (P(None, ("wide", "narrow")), P(), P())
    out_specs = P(None, ("wide", "narrow"))
    return jax.shard_map(local, mesh=mesh, in_specs=in_specs, out_specs=out_specs, check_vma=False)
```

```python
import functools
import math

import jax
import jax.numpy as jnp
from jax import lax
from jax.experimental import pallas as pl
from jax.experimental.pallas import tpu as pltpu
from jax.sharding import PartitionSpec as P

GATE = 128

angle_step = 2.0 * math.pi / 256.0


def split(value):
    high = value.astype(jnp.bfloat16)
    low = (value - high.astype(jnp.float32)).astype(jnp.bfloat16)
    return high, low


def product(left, right):
    (left_high, left_low), (right_high, right_low) = left, right
    dot = functools.partial(jnp.dot, preferred_element_type=jnp.float32)
    return dot(left_high, right_high) + (dot(left_high, right_low) + dot(left_low, right_high))


def real_form(gate_re, gate_im):
    upper = jnp.concatenate([gate_re, -gate_im], axis=1)
    lower = jnp.concatenate([gate_im, gate_re], axis=1)
    return jnp.concatenate([upper, lower], axis=0)


def kernel(
    dims,
    x_ref,
    gates_in,
    phase_index_ref,
    out_ref,
    amps,
    gates_ref,
    gate_rows,
    spread,
    gathered,
    finished,
    returned,
    own_sem,
    gates_sem,
    staged,
    out_sem,
    swap_send,
    swap_recv,
    spread_send,
    spread_recv,
    return_send,
    return_recv,
):
    wide_count, narrow_count, chunk_count, free, extra, inner, low, per_dest, top_span = dims
    wide = lax.axis_index("wide")
    me = lax.axis_index("narrow")
    side = wide // (wide_count // 2)
    partner = lax.rem(wide + wide_count // 2, wide_count)
    sides = (wide, partner)
    half = GATE // 2

    def swap(c):
        return pltpu.make_async_remote_copy(
            src_ref=x_ref.at[1 - side, c],
            dst_ref=amps.at[1, c],
            send_sem=swap_send.at[c],
            recv_sem=swap_recv.at[c],
            device_id=(partner, me),
            device_id_type=pl.DeviceIdType.MESH,
        )

    def spread_copy(slot, f, d):
        dest = lax.rem(me + d, narrow_count)
        return pltpu.make_async_remote_copy(
            src_ref=spread.at[slot, f, dest],
            dst_ref=gathered.at[slot, f, me],
            send_sem=spread_send.at[slot, f, d],
            recv_sem=spread_recv.at[slot, f, me],
            device_id=(wide, dest),
            device_id_type=pl.DeviceIdType.MESH,
        )

    def spread_arrival(slot, f, d):
        source = lax.rem(me + d, narrow_count)
        return pltpu.make_async_remote_copy(
            src_ref=spread.at[slot, f, source],
            dst_ref=gathered.at[slot, f, source],
            send_sem=spread_send.at[slot, f, d],
            recv_sem=spread_recv.at[slot, f, source],
            device_id=(wide, source),
            device_id_type=pl.DeviceIdType.MESH,
        )

    def return_copy(slot, f, d):
        dest = lax.rem(me + d, narrow_count)
        return pltpu.make_async_remote_copy(
            src_ref=finished.at[slot, f, dest],
            dst_ref=returned.at[slot, f, me],
            send_sem=return_send.at[slot, f, d],
            recv_sem=return_recv.at[slot, f, me],
            device_id=(sides[slot], dest),
            device_id_type=pl.DeviceIdType.MESH,
        )

    def return_arrival(slot, f, d):
        source = lax.rem(me + d, narrow_count)
        return pltpu.make_async_remote_copy(
            src_ref=finished.at[slot, f, source],
            dst_ref=returned.at[slot, f, source],
            send_sem=return_send.at[slot, f, d],
            recv_sem=return_recv.at[slot, f, source],
            device_id=(sides[slot], source),
            device_id_type=pl.DeviceIdType.MESH,
        )

    own = pltpu.make_async_copy(x_ref.at[side], amps.at[0], own_sem)
    own.start()
    gates_copy = pltpu.make_async_copy(gates_in, gates_ref, gates_sem)
    gates_copy.start()
    barrier = pltpu.get_barrier_semaphore()
    for slot in range(2):
        for d in range(1 - slot, narrow_count):
            peer = lax.rem(me + d, narrow_count)
            pl.semaphore_signal(
                barrier, inc=1, device_id=(sides[slot], peer), device_id_type=pl.DeviceIdType.MESH
            )
    pl.semaphore_wait(barrier, 2 * narrow_count - 1)
    window = min(3, chunk_count)
    for c in range(window):
        swap(c).start()

    angles = phase_index_ref[...].astype(jnp.float32) * angle_step
    cosine, sine = jnp.cos(angles), jnp.sin(angles)
    gates_copy.wait()

    cos_low, sin_low = cosine[0:1, :], sine[0:1, :]
    re, im = gates_ref[0, 0].T, gates_ref[0, 1].T
    re, im = re * cos_low - im * sin_low, re * sin_low + im * cos_low
    upper = jnp.concatenate([re, im], axis=1)
    lower = jnp.concatenate([-im, re], axis=1)
    lane_gate = split(jnp.concatenate([upper, lower], axis=0))

    cos_mid = jnp.broadcast_to(cosine[1:2, :], (GATE, GATE)).T
    sin_mid = jnp.broadcast_to(sine[1:2, :], (GATE, GATE)).T
    re, im = gates_ref[1, 0], gates_ref[1, 1]
    gate_rows[0] = re * cos_mid - im * sin_mid
    gate_rows[1] = re * sin_mid + im * cos_mid

    def row_start(s):
        return (s // low) * low * inner + s % low

    settings = GATE // inner
    re, im = [
        jnp.concatenate(
            [gate_rows[p, pl.ds(row_start(s), inner, stride=low), :] for s in range(settings)], axis=0
        )
        for p in range(2)
    ]
    row_gate = split(real_form(re, im))

    lanes = lax.broadcasted_iota(jnp.int32, (1, GATE), 1)

    def first_gates(slot, c):
        x = jnp.concatenate([amps[slot, c, pl.ds(p, GATE, stride=2), :] for p in range(2)], axis=0)
        y = product(row_gate, split(x))
        y = jnp.concatenate([y[:GATE], y[GATE:]], axis=1)
        y = product(split(y), lane_gate)
        re, im = y[:, :GATE], y[:, GATE:]
        device = sides[slot] * narrow_count + me
        top = ((device * 2 + side) * chunk_count + c) // top_span
        cos_top = jnp.sum(jnp.where(lanes == top, cosine[2:3, :], 0.0), axis=1, keepdims=True)
        sin_top = jnp.sum(jnp.where(lanes == top, sine[2:3, :], 0.0), axis=1, keepdims=True)
        f, e = c // extra, c % extra
        shape = (narrow_count, per_dest * inner, GATE)
        spread[slot, f, :, e, 0] = (re * cos_top - im * sin_top).reshape(shape)
        spread[slot, f, :, e, 1] = (re * sin_top + im * cos_top).reshape(shape)
        if e == extra - 1:
            for d in range(1, narrow_count):
                spread_copy(slot, f, d).start()
            gathered[slot, f, me] = spread[slot, f, me]

    own.wait()
    for c in range(extra):
        first_gates(0, c)

    third_gate = split(real_form(gates_ref[2, 0], gates_ref[2, 1]))

    def by_side(gate):
        turned = jnp.concatenate([gate[:, half:], gate[:, :half]], axis=1)
        turned = jnp.concatenate([turned[half:], turned[:half]], axis=0)
        return jnp.where(side == 0, gate, turned)

    fourth_gate = split(real_form(by_side(gates_ref[3, 0]), by_side(gates_ref[3, 1])))

    def last_gates(f):
        ys = []
        for slot in range(2):
            for d in range(1, narrow_count):
                spread_arrival(slot, f, d).wait_recv()
            columns = [
                jnp.concatenate(
                    [
                        gathered[slot, f, n, e, p, u * inner : (u + 1) * inner, :]
                        for p in range(2)
                        for n in range(narrow_count)
                        for e in range(extra)
                    ],
                    axis=0,
                )
                for u in range(per_dest)
            ]
            x = jnp.concatenate(columns, axis=1) if per_dest > 1 else columns[0]
            ys.append(product(third_gate, split(x)))
        for t in range(2):
            x = jnp.concatenate(
                [
                    ys[slot][p * GATE + t * half : p * GATE + (t + 1) * half]
                    for p in range(2)
                    for slot in range(2)
                ],
                axis=0,
            )
            z = product(fourth_gate, split(x))
            for slot in range(2):
                for n in range(narrow_count // 2):
                    for e in range(extra):
                        for p in range(2):
                            row = p * GATE + slot * half + (n * extra + e) * inner
                            for u in range(per_dest):
                                finished[
                                    slot, f, t * (narrow_count // 2) + n, e, p, u * inner : (u + 1) * inner, :
                                ] = z[row : row + inner, u * GATE : (u + 1) * GATE]
        for slot in (1, 0):
            for d in range(1 - slot, narrow_count):
                return_copy(slot, f, d).start()
        returned[0, f, me] = finished[0, f, me]

    for f in range(free):
        if f > 0:
            for e in range(extra):
                first_gates(0, f * extra + e)
        for e in range(extra):
            c = f * extra + e
            swap(c).wait_recv()
            if c + window < chunk_count:
                swap(c + window).start()
            first_gates(1, c)
        last_gates(f)

    def store(slot, f):
        origin = side if slot == 0 else 1 - side
        part = pl.ds(f * extra, extra)
        return pltpu.make_async_copy(staged.at[origin, part], out_ref.at[origin, part], out_sem.at[f, slot])

    for f in range(free):
        for slot in range(2):
            for d in range(1 - slot, narrow_count):
                return_arrival(slot, f, d).wait_recv()
            origin = side if slot == 0 else 1 - side
            for n in range(narrow_count):
                for e in range(extra):
                    for p in range(2):
                        for u in range(per_dest):
                            row = 2 * row_start(n * per_dest + u) + p
                            staged[origin, f * extra + e, pl.ds(row, inner, stride=2 * low), :] = returned[
                                slot, f, n, e, p, u * inner : (u + 1) * inner, :
                            ]

            store(slot, f).start()

    for c in range(chunk_count):
        swap(c).wait_send()
    for f in range(free):
        for slot in range(2):
            for d in range(1, narrow_count):
                spread_copy(slot, f, d).wait_send()
            for d in range(1 - slot, narrow_count):
                return_copy(slot, f, d).wait_send()
            store(slot, f).wait()


def local(state, gates, phase_index):
    local_amps = state.shape[1]
    narrow_count = lax.axis_size("narrow")
    wide_count = lax.axis_size("wide")
    rows = local_amps // GATE
    low = rows // GATE
    chunk_count = local_amps // (2 * GATE * GATE)
    contracted = GATE // narrow_count
    inner = min(contracted, GATE // low)
    extra = contracted // inner
    free = chunk_count // extra
    per_dest = GATE // inner // narrow_count
    top_span = local_amps * wide_count * narrow_count // GATE**3
    dims = (wide_count, narrow_count, chunk_count, free, extra, inner, low, per_dest, top_span)
    x = state.reshape(2, rows, GATE).transpose(1, 0, 2).reshape(2, chunk_count, 2 * GATE, GATE)
    vmem = pl.BlockSpec(memory_space=pltpu.VMEM)
    hbm = pl.BlockSpec(memory_space=pltpu.HBM)
    message = pltpu.VMEM((2, free, narrow_count, extra, 2, per_dest * inner, GATE), jnp.float32)
    pair_sems = pltpu.SemaphoreType.DMA((2, free, narrow_count))
    flops = 4 * 2 * (2 * GATE) ** 2 * rows * 3
    out = pl.pallas_call(
        functools.partial(kernel, dims),
        out_shape=jax.ShapeDtypeStruct(x.shape, jnp.float32),
        in_specs=[hbm, hbm, vmem],
        out_specs=hbm,
        scratch_shapes=[
            pltpu.VMEM(x.shape, jnp.float32),
            pltpu.VMEM(gates.shape, jnp.float32),
            pltpu.VMEM((2, GATE, GATE), jnp.float32),
            message,
            message,
            message,
            message,
            pltpu.SemaphoreType.DMA,
            pltpu.SemaphoreType.DMA,
            pltpu.VMEM(x.shape, jnp.float32),
            pltpu.SemaphoreType.DMA((free, 2)),
            pltpu.SemaphoreType.DMA((chunk_count,)),
            pltpu.SemaphoreType.DMA((chunk_count,)),
            pair_sems,
            pair_sems,
            pair_sems,
            pair_sems,
        ],
        compiler_params=pltpu.CompilerParams(
            collective_id=0, has_side_effects=True, vmem_limit_bytes=60 * 2**20
        ),
        cost_estimate=pl.CostEstimate(flops=flops, bytes_accessed=4 * local_amps * 4, transcendentals=0),
    )(x, gates, phase_index)
    return out.reshape(rows, 2, GATE).transpose(1, 0, 2).reshape(2, local_amps)


def solution(mesh):
    in_specs = (P(None, ("wide", "narrow")), P(), P())
    out_specs = P(None, ("wide", "narrow"))
    return jax.shard_map(local, mesh=mesh, in_specs=in_specs, out_specs=out_specs, check_vma=False)
```

```python
import functools
import math

import jax
import jax.numpy as jnp
from jax import lax
from jax.experimental import pallas as pl
from jax.experimental.pallas import tpu as pltpu
from jax.sharding import PartitionSpec as P

GATE = 128

angle_step = 2.0 * math.pi / 256.0


def split(value):
    high = value.astype(jnp.bfloat16)
    low = (value - high.astype(jnp.float32)).astype(jnp.bfloat16)
    return high, low


def product(left, right):
    (left_high, left_low), (right_high, right_low) = left, right
    dot = functools.partial(jnp.dot, preferred_element_type=jnp.float32)
    return dot(left_high, right_high) + (dot(left_high, right_low) + dot(left_low, right_high))


def real_form(gate_re, gate_im):
    upper = jnp.concatenate([gate_re, -gate_im], axis=1)
    lower = jnp.concatenate([gate_im, gate_re], axis=1)
    return jnp.concatenate([upper, lower], axis=0)


def kernel(
    dims,
    x_ref,
    gates_in,
    phase_index_ref,
    out_ref,
    amps,
    gates_ref,
    gate_rows,
    spread,
    gathered,
    finished,
    returned,
    own_sem,
    gates_sem,
    staged,
    out_sem,
    swap_send,
    swap_recv,
    spread_send,
    spread_recv,
    return_send,
    return_recv,
):
    wide_count, narrow_count, chunk_count, free, extra, inner, low, per_dest, top_span = dims
    wide = lax.axis_index("wide")
    me = lax.axis_index("narrow")
    side = wide // (wide_count // 2)
    partner = lax.rem(wide + wide_count // 2, wide_count)
    sides = (wide, partner)
    half = GATE // 2

    def swap(c):
        return pltpu.make_async_remote_copy(
            src_ref=x_ref.at[1 - side, c],
            dst_ref=amps.at[1, c],
            send_sem=swap_send.at[c],
            recv_sem=swap_recv.at[c],
            device_id=(partner, me),
            device_id_type=pl.DeviceIdType.MESH,
        )

    def spread_copy(slot, f, e, d):
        dest = lax.rem(me + d, narrow_count)
        return pltpu.make_async_remote_copy(
            src_ref=spread.at[slot, f, dest, e],
            dst_ref=gathered.at[slot, f, me, e],
            send_sem=spread_send.at[slot, f, e, d],
            recv_sem=spread_recv.at[slot, f, e, me],
            device_id=(wide, dest),
            device_id_type=pl.DeviceIdType.MESH,
        )

    def spread_arrival(slot, f, e, d):
        source = lax.rem(me + d, narrow_count)
        return pltpu.make_async_remote_copy(
            src_ref=spread.at[slot, f, source, e],
            dst_ref=gathered.at[slot, f, source, e],
            send_sem=spread_send.at[slot, f, e, d],
            recv_sem=spread_recv.at[slot, f, e, source],
            device_id=(wide, source),
            device_id_type=pl.DeviceIdType.MESH,
        )

    def return_copy(slot, f, d):
        dest = lax.rem(me + d, narrow_count)
        return pltpu.make_async_remote_copy(
            src_ref=finished.at[slot, f, dest],
            dst_ref=returned.at[slot, f, me],
            send_sem=return_send.at[slot, f, d],
            recv_sem=return_recv.at[slot, f, me],
            device_id=(sides[slot], dest),
            device_id_type=pl.DeviceIdType.MESH,
        )

    def return_arrival(slot, f, d):
        source = lax.rem(me + d, narrow_count)
        return pltpu.make_async_remote_copy(
            src_ref=finished.at[slot, f, source],
            dst_ref=returned.at[slot, f, source],
            send_sem=return_send.at[slot, f, d],
            recv_sem=return_recv.at[slot, f, source],
            device_id=(sides[slot], source),
            device_id_type=pl.DeviceIdType.MESH,
        )

    own = pltpu.make_async_copy(x_ref.at[side], amps.at[0], own_sem)
    own.start()
    gates_copy = pltpu.make_async_copy(gates_in, gates_ref, gates_sem)
    gates_copy.start()
    barrier = pltpu.get_barrier_semaphore()
    for slot in range(2):
        for d in range(1 - slot, narrow_count):
            peer = lax.rem(me + d, narrow_count)
            pl.semaphore_signal(
                barrier, inc=1, device_id=(sides[slot], peer), device_id_type=pl.DeviceIdType.MESH
            )
    pl.semaphore_wait(barrier, 2 * narrow_count - 1)
    window = min(3, chunk_count)
    for c in range(window):
        swap(c).start()

    angles = phase_index_ref[...].astype(jnp.float32) * angle_step
    cosine, sine = jnp.cos(angles), jnp.sin(angles)
    gates_copy.wait()

    cos_low, sin_low = cosine[0:1, :], sine[0:1, :]
    re, im = gates_ref[0, 0].T, gates_ref[0, 1].T
    re, im = re * cos_low - im * sin_low, re * sin_low + im * cos_low
    upper = jnp.concatenate([re, im], axis=1)
    lower = jnp.concatenate([-im, re], axis=1)
    lane_gate = split(jnp.concatenate([upper, lower], axis=0))

    cos_mid = jnp.broadcast_to(cosine[1:2, :], (GATE, GATE)).T
    sin_mid = jnp.broadcast_to(sine[1:2, :], (GATE, GATE)).T
    re, im = gates_ref[1, 0], gates_ref[1, 1]
    gate_rows[0] = re * cos_mid - im * sin_mid
    gate_rows[1] = re * sin_mid + im * cos_mid

    def row_start(s):
        return (s // low) * low * inner + s % low

    settings = GATE // inner
    re, im = [
        jnp.concatenate(
            [gate_rows[p, pl.ds(row_start(s), inner, stride=low), :] for s in range(settings)], axis=0
        )
        for p in range(2)
    ]
    row_gate = split(real_form(re, im))

    lanes = lax.broadcasted_iota(jnp.int32, (1, GATE), 1)

    def first_gates(slot, c):
        x = jnp.concatenate([amps[slot, c, pl.ds(p, GATE, stride=2), :] for p in range(2)], axis=0)
        y = product(row_gate, split(x))
        y = jnp.concatenate([y[:GATE], y[GATE:]], axis=1)
        y = product(split(y), lane_gate)
        re, im = y[:, :GATE], y[:, GATE:]
        device = sides[slot] * narrow_count + me
        top = ((device * 2 + side) * chunk_count + c) // top_span
        cos_top = jnp.sum(jnp.where(lanes == top, cosine[2:3, :], 0.0), axis=1, keepdims=True)
        sin_top = jnp.sum(jnp.where(lanes == top, sine[2:3, :], 0.0), axis=1, keepdims=True)
        f, e = c // extra, c % extra
        shape = (narrow_count, per_dest * inner, GATE)
        spread[slot, f, :, e, 0] = (re * cos_top - im * sin_top).reshape(shape)
        spread[slot, f, :, e, 1] = (re * sin_top + im * cos_top).reshape(shape)
        for d in range(1, narrow_count):
            spread_copy(slot, f, e, d).start()
        gathered[slot, f, me, e] = spread[slot, f, me, e]

    own.wait()
    for c in range(extra):
        first_gates(0, c)

    third_gate = split(real_form(gates_ref[2, 0], gates_ref[2, 1]))

    def by_side(gate):
        turned = jnp.concatenate([gate[:, half:], gate[:, :half]], axis=1)
        turned = jnp.concatenate([turned[half:], turned[:half]], axis=0)
        return jnp.where(side == 0, gate, turned)

    fourth_gate = split(real_form(by_side(gates_ref[3, 0]), by_side(gates_ref[3, 1])))

    def last_gates(f):
        ys = []
        for slot in range(2):
            for d in range(1, narrow_count):
                for e in range(extra):
                    spread_arrival(slot, f, e, d).wait_recv()
            columns = [
                jnp.concatenate(
                    [
                        gathered[slot, f, n, e, p, u * inner : (u + 1) * inner, :]
                        for p in range(2)
                        for n in range(narrow_count)
                        for e in range(extra)
                    ],
                    axis=0,
                )
                for u in range(per_dest)
            ]
            x = jnp.concatenate(columns, axis=1) if per_dest > 1 else columns[0]
            ys.append(product(third_gate, split(x)))
        for t in range(2):
            x = jnp.concatenate(
                [
                    ys[slot][p * GATE + t * half : p * GATE + (t + 1) * half]
                    for p in range(2)
                    for slot in range(2)
                ],
                axis=0,
            )
            z = product(fourth_gate, split(x))
            for slot in range(2):
                for n in range(narrow_count // 2):
                    for e in range(extra):
                        for p in range(2):
                            row = p * GATE + slot * half + (n * extra + e) * inner
                            for u in range(per_dest):
                                finished[
                                    slot, f, t * (narrow_count // 2) + n, e, p, u * inner : (u + 1) * inner, :
                                ] = z[row : row + inner, u * GATE : (u + 1) * GATE]
        for slot in (1, 0):
            for d in range(1 - slot, narrow_count):
                return_copy(slot, f, d).start()
        returned[0, f, me] = finished[0, f, me]

    for f in range(free):
        if f > 0:
            for e in range(extra):
                first_gates(0, f * extra + e)
        for e in range(extra):
            c = f * extra + e
            swap(c).wait_recv()
            if c + window < chunk_count:
                swap(c + window).start()
            first_gates(1, c)
        last_gates(f)

    def store(slot, f):
        origin = side if slot == 0 else 1 - side
        part = pl.ds(f * extra, extra)
        return pltpu.make_async_copy(staged.at[origin, part], out_ref.at[origin, part], out_sem.at[f, slot])

    for f in range(free):
        for slot in range(2):
            for d in range(1 - slot, narrow_count):
                return_arrival(slot, f, d).wait_recv()
            origin = side if slot == 0 else 1 - side
            for n in range(narrow_count):
                for e in range(extra):
                    for p in range(2):
                        for u in range(per_dest):
                            row = 2 * row_start(n * per_dest + u) + p
                            staged[origin, f * extra + e, pl.ds(row, inner, stride=2 * low), :] = returned[
                                slot, f, n, e, p, u * inner : (u + 1) * inner, :
                            ]

            store(slot, f).start()

    for c in range(chunk_count):
        swap(c).wait_send()
    for f in range(free):
        for slot in range(2):
            for d in range(1, narrow_count):
                for e in range(extra):
                    spread_copy(slot, f, e, d).wait_send()
            for d in range(1 - slot, narrow_count):
                return_copy(slot, f, d).wait_send()
            store(slot, f).wait()


def local(state, gates, phase_index):
    local_amps = state.shape[1]
    narrow_count = lax.axis_size("narrow")
    wide_count = lax.axis_size("wide")
    rows = local_amps // GATE
    low = rows // GATE
    chunk_count = local_amps // (2 * GATE * GATE)
    contracted = GATE // narrow_count
    inner = min(contracted, GATE // low)
    extra = contracted // inner
    free = chunk_count // extra
    per_dest = GATE // inner // narrow_count
    top_span = local_amps * wide_count * narrow_count // GATE**3
    dims = (wide_count, narrow_count, chunk_count, free, extra, inner, low, per_dest, top_span)
    x = state.reshape(2, rows, GATE).transpose(1, 0, 2).reshape(2, chunk_count, 2 * GATE, GATE)
    vmem = pl.BlockSpec(memory_space=pltpu.VMEM)
    hbm = pl.BlockSpec(memory_space=pltpu.HBM)
    message = pltpu.VMEM((2, free, narrow_count, extra, 2, per_dest * inner, GATE), jnp.float32)
    piece_sems = pltpu.SemaphoreType.DMA((2, free, extra, narrow_count))
    pair_sems = pltpu.SemaphoreType.DMA((2, free, narrow_count))
    flops = 4 * 2 * (2 * GATE) ** 2 * rows * 3
    out = pl.pallas_call(
        functools.partial(kernel, dims),
        out_shape=jax.ShapeDtypeStruct(x.shape, jnp.float32),
        in_specs=[hbm, hbm, vmem],
        out_specs=hbm,
        scratch_shapes=[
            pltpu.VMEM(x.shape, jnp.float32),
            pltpu.VMEM(gates.shape, jnp.float32),
            pltpu.VMEM((2, GATE, GATE), jnp.float32),
            message,
            message,
            message,
            message,
            pltpu.SemaphoreType.DMA,
            pltpu.SemaphoreType.DMA,
            pltpu.VMEM(x.shape, jnp.float32),
            pltpu.SemaphoreType.DMA((free, 2)),
            pltpu.SemaphoreType.DMA((chunk_count,)),
            pltpu.SemaphoreType.DMA((chunk_count,)),
            piece_sems,
            piece_sems,
            pair_sems,
            pair_sems,
        ],
        compiler_params=pltpu.CompilerParams(
            collective_id=0, has_side_effects=True, vmem_limit_bytes=60 * 2**20
        ),
        cost_estimate=pl.CostEstimate(flops=flops, bytes_accessed=4 * local_amps * 4, transcendentals=0),
    )(x, gates, phase_index)
    return out.reshape(rows, 2, GATE).transpose(1, 0, 2).reshape(2, local_amps)


def solution(mesh):
    in_specs = (P(None, ("wide", "narrow")), P(), P())
    out_specs = P(None, ("wide", "narrow"))
    return jax.shard_map(local, mesh=mesh, in_specs=in_specs, out_specs=out_specs, check_vma=False)
```
